32 devices in a mesh: ctx: 8 (over y, x, core), head: 4 (over z).
Axes of the slice: x: 2, y: 2, z: 4, core: 2. Of those that a mesh axis runs over, the one named last changes fastest.
Arguments:
- queries: bfloat16 [8192, 4096], P(('ctx', 'head')), may hold values from -6 to 6
- keys: bfloat16 [8192, 4096], P(('ctx', 'head')), may hold values from -6 to 6
- values: bfloat16 [8192, 4096], P(('ctx', 'head')), may hold values from -6 to 6
- out_grad: bfloat16 [8192, 4096], P(('ctx', 'head')), may hold values from -1024 to 1024, as said below
Outputs:
- grad_queries: bfloat16 [8192, 4096], P(('ctx', 'head'))
- grad_keys: bfloat16 [8192, 4096], P(('ctx', 'head'))
- grad_values: bfloat16 [8192, 4096], P(('ctx', 'head'))
The draws below stay inside these ranges and needn't reach their ends.
Inputs may be any that keep to these rules, and one draw needn't show every extreme that they name: `out_grad`: output gradients of varying size along the sequence.
All inputs are finite; a program needn't handle non-finite values.
Results may differ from the reference program's by a relative error of at most 0.011.
Values may be sent and summed in bfloat16 or wider, within the bound.
A program may use at most 128 MiB of HBM per device.

```python
import jax
import jax.numpy as jnp
from jax import lax

HEADS = 32
HD = 128
BLOCK = 512
SEQ = 8192


def draw_out_grad(key, part):
    noise = jnp.clip(jax.random.normal(key, (SEQ, HEADS * HD), jnp.float32), -4.0, 4.0)
    rising = 2.0 * jnp.sqrt(jnp.arange(SEQ, dtype=jnp.float32) + 1.0)
    return jnp.clip(noise * rising[:, None], -1024.0, 1024.0).astype(jnp.bfloat16)


def shard_levels(key, dims, split, least, top_value):
    gain = 1.0
    for position, shards_of in split:
        draws = jax.random.uniform(jax.random.fold_in(jax.random.fold_in(key, 6), position), (shards_of,), jnp.float32, least / len(split), top_value / len(split))
        gain = gain * jnp.repeat(jnp.exp(draws), dims[position] // shards_of).reshape((-1,) + (1,) * (len(dims) - 1 - position))
    return gain


def bell_draw(stream_key, shape, width, reach, pieces=(), kind=jnp.bfloat16):
    level = shard_levels(stream_key, shape, pieces, -0.22, 0.18) if pieces else 1.0
    array = jax.random.normal(stream_key, shape, jnp.float32) * width * level
    return jnp.minimum(jnp.maximum(array, -reach), reach).astype(kind)


def setup_inputs(seed: int = 0) -> dict:
    key_list = jax.random.split(jax.random.key(seed), 5)
    queries = bell_draw(key_list[0], (SEQ, HEADS * HD), 1.0, 6.0, ((0, 32),))
    keys = bell_draw(key_list[1], (SEQ, HEADS * HD), 1.0, 6.0, ((0, 32),))
    values = bell_draw(key_list[2], (SEQ, HEADS * HD), 1.0, 6.0, ((0, 32),))
    out_grad = draw_out_grad(jax.random.fold_in(key_list[4], 71), 0)
    return dict(queries=queries, keys=keys, values=values, out_grad=out_grad)


def feature(inputs):
    real = inputs.astype(jnp.float32)
    return jnp.where(real > 0, real + 1.0, jnp.exp(jnp.minimum(real, 0.0)))


def slope(inputs):
    real = inputs.astype(jnp.float32)
    return jnp.where(real > 0, 1.0, jnp.exp(jnp.minimum(real, 0.0)))


def forward_block(query_feat, key_feat, value_rows, grad_rows, prefix_state, prefix_sum):
    length = query_feat.shape[0]
    causal = jnp.arange(length)[:, None] >= jnp.arange(length)[None, :]
    scores = jnp.where(causal, jnp.dot(query_feat, key_feat.T, preferred_element_type=jnp.float32), 0.0)
    weights = scores.astype(jnp.bfloat16)
    state_half = prefix_state.astype(jnp.bfloat16)
    numerator = jnp.dot(weights, value_rows, preferred_element_type=jnp.float32) + jnp.dot(query_feat, state_half, preferred_element_type=jnp.float32)
    denominator = jnp.sum(scores, axis=1) + jnp.dot(query_feat.astype(jnp.float32), prefix_sum, precision=lax.Precision.HIGHEST)
    attended = numerator / denominator[:, None]
    grad_real = grad_rows.astype(jnp.float32)
    grad_numerator = (grad_real / denominator[:, None]).astype(jnp.bfloat16)
    grad_denominator = -jnp.sum(grad_real * attended, axis=1) / denominator
    mixing = jnp.where(causal, jnp.dot(grad_numerator, value_rows.T, preferred_element_type=jnp.float32) + grad_denominator[:, None], 0.0).astype(jnp.bfloat16)
    grad_query_feat = jnp.dot(mixing, key_feat, preferred_element_type=jnp.float32) + jnp.dot(grad_numerator, state_half.T, preferred_element_type=jnp.float32) + grad_denominator[:, None] * prefix_sum[None, :]
    return grad_query_feat, grad_numerator, grad_denominator


def backward_block(query_feat, key_feat, value_rows, grad_numerator, grad_denominator, suffix_state, suffix_sum):
    length = query_feat.shape[0]
    causal = jnp.arange(length)[:, None] >= jnp.arange(length)[None, :]
    scores = jnp.where(causal, jnp.dot(query_feat, key_feat.T, preferred_element_type=jnp.float32), 0.0)
    weights = scores.astype(jnp.bfloat16)
    mixing = jnp.where(causal, jnp.dot(grad_numerator, value_rows.T, preferred_element_type=jnp.float32) + grad_denominator[:, None], 0.0).astype(jnp.bfloat16)
    state_half = suffix_state.astype(jnp.bfloat16)
    grad_key_feat = jnp.dot(mixing.T, query_feat, preferred_element_type=jnp.float32) + jnp.dot(value_rows, state_half.T, preferred_element_type=jnp.float32) + suffix_sum[None, :]
    grad_value = jnp.dot(weights.T, grad_numerator, preferred_element_type=jnp.float32) + jnp.dot(key_feat, state_half, preferred_element_type=jnp.float32)
    return grad_key_feat, grad_value.astype(jnp.bfloat16)


def per_head(inputs):
    query_rows, key_rows, value_rows, grad_rows = inputs
    query_feat = feature(query_rows).astype(jnp.bfloat16)
    key_feat = feature(key_rows).astype(jnp.bfloat16)

    def forward_step(carry, blocks):
        prefix_state, prefix_sum = carry
        query_blk, key_blk, value_blk, grad_blk = blocks
        outputs = forward_block(query_blk, key_blk, value_blk, grad_blk, prefix_state, prefix_sum)
        update = jnp.dot(key_blk.T, value_blk, preferred_element_type=jnp.float32)
        key_total = jnp.sum(key_blk.astype(jnp.float32), axis=0)
        return (prefix_state + update, prefix_sum + key_total), outputs

    start_state = (jnp.zeros((HD, HD), jnp.float32), jnp.zeros((HD,), jnp.float32))
    ignored, forward_out = lax.scan(forward_step, start_state, (query_feat, key_feat, value_rows, grad_rows))
    grad_query_feat, grad_numerator, grad_denominator = forward_out

    def backward_step(carry, blocks):
        suffix_state, suffix_sum = carry
        query_blk, key_blk, value_blk, numer_blk, denom_blk = blocks
        outputs = backward_block(query_blk, key_blk, value_blk, numer_blk, denom_blk, suffix_state, suffix_sum)
        update = jnp.dot(query_blk.T, numer_blk, preferred_element_type=jnp.float32)
        query_total = jnp.sum(denom_blk[:, None] * query_blk.astype(jnp.float32), axis=0)
        return (suffix_state + update, suffix_sum + query_total), outputs

    ignored, backward_out = lax.scan(backward_step, start_state, (query_feat, key_feat, value_rows, grad_numerator, grad_denominator), reverse=True)
    grad_key_feat, grad_value = backward_out
    grad_query = (grad_query_feat * slope(query_rows)).astype(jnp.bfloat16)
    grad_key = (grad_key_feat * slope(key_rows)).astype(jnp.bfloat16)
    return grad_query, grad_key, grad_value


def reference(queries, keys, values, out_grad):
    def heads_first(inputs):
        return inputs.reshape(SEQ // BLOCK, BLOCK, HEADS, HD).transpose(2, 0, 1, 3)

    def tokens_first(inputs):
        return inputs.transpose(1, 2, 0, 3).reshape(SEQ, HEADS * HD)

    results = lax.map(per_head, (heads_first(queries), heads_first(keys), heads_first(values), heads_first(out_grad)))
    return tokens_first(results[0]), tokens_first(results[1]), tokens_first(results[2])
```

```python
import functools

import jax
import jax.numpy as jnp
from jax import lax
from jax.experimental import pallas as pl
from jax.experimental.pallas import tpu as pltpu
from jax.sharding import PartitionSpec as P

HD = 128
CH = 2
F32 = jnp.float32
BF16 = jnp.bfloat16
MESH = pl.DeviceIdType.MESH


def dot(a, b, ca, cb):
    return lax.dot_general(a, b, (((ca,), (cb,)), ((), ())), preferred_element_type=F32)


def kernel(nctx, nz, q, k, v, g, gq, gk, gv, fq, fk, dn, w, dfk, den_all, u, snd, rcv,
           avec, zpre, cvec, rpre, vrcv, zsnd, zrcv, ss, rs, vss, vrs, zss, zrs):
    T = q.shape[0]
    H = q.shape[1] // HD
    NC = H // CH
    nb = nctx.bit_length() - 1
    NS = nb + nz - 1
    VB, VC, D1 = 1, 2, 2
    c = lax.axis_index("ctx")
    z = lax.axis_index("head")

    barrier = pltpu.get_barrier_semaphore()
    for o in range(1, nctx):
        pl.semaphore_signal(barrier, inc=1, device_id=(lax.rem(c + o, nctx), z), device_id_type=MESH)
    for o in range(1, nz):
        pl.semaphore_signal(barrier, inc=1, device_id=(c, lax.rem(z + o, nz)), device_id_type=MESH)
    pl.semaphore_wait(barrier, nctx + nz - 2)

    bits = [lax.rem(c // (1 << s), 2) for s in range(nb)]

    def cols(h):
        return pl.ds(pl.multiple_of(h * HD, HD), HD)

    def vec_ctx(d, o, src):
        return pltpu.make_async_remote_copy(
            src_ref=src, dst_ref=vrcv.at[d, c], send_sem=vss.at[d, o], recv_sem=vrs.at[d, c],
            device_id=(lax.rem(c + o, nctx), z), device_id_type=MESH)

    def vec_ctx_from(d, o, src):
        p = lax.rem(c + o, nctx)
        return p, pltpu.make_async_remote_copy(
            src_ref=src, dst_ref=vrcv.at[d, p], send_sem=vss.at[d, o], recv_sem=vrs.at[d, p],
            device_id=(p, z), device_id_type=MESH)

    def vec_z(d, o, which):
        return pltpu.make_async_remote_copy(
            src_ref=zsnd.at[d, which], dst_ref=zrcv.at[d, z], send_sem=zss.at[d, o], recv_sem=zrs.at[d, z],
            device_id=(c, lax.rem(z + o, nz)), device_id_type=MESH)

    def vec_z_from(d, o):
        p = lax.rem(z + o, nz)
        return p, pltpu.make_async_remote_copy(
            src_ref=zsnd.at[d, 0], dst_ref=zrcv.at[d, p], send_sem=zss.at[d, o], recv_sem=zrs.at[d, p],
            device_id=(c, p), device_id_type=MESH)

    def vec_start(d, src):
        for o in range(1, nctx):
            vec_ctx(d, o, src).start()

    def vec_middle(d, src, out):
        total = jnp.zeros((H, HD), F32)
        for o in range(1, nctx):
            p, copy = vec_ctx_from(d, o, src)
            copy.wait_recv()
            take = (p < c) if d == 0 else (p > c)
            total = total + jnp.where(take, vrcv[d, p], 0.0)
        out[...] = total
        zsnd[d, 0] = total + src[...]
        zsnd[d, 1] = total
        for o in range(1, nz):
            ahead = lax.rem(z + o, nz) > z
            which = jnp.where(ahead, 0, 1) if d == 0 else jnp.where(ahead, 1, 0)
            vec_z(d, o, which).start()

    def vec_end(d, src, out):
        total = out[...]
        for o in range(1, nz):
            p, copy = vec_z_from(d, o)
            copy.wait_recv()
            total = total + zrcv[d, p]
        out[...] = total

    def state_copy(d, s, j):
        if s < nb:
            dev = (c + (1 - 2 * bits[s]) * (1 << s), z)
        else:
            up = (s == nb) == (d == 0)
            dev = (c, jnp.clip(z + 1, 0, nz - 1) if up else jnp.clip(z - 1, 0, nz - 1))
        return pltpu.make_async_remote_copy(
            src_ref=snd.at[d, s, j], dst_ref=rcv.at[d, s, j], send_sem=ss.at[d, s, j],
            recv_sem=rs.at[d, s, j], device_id=dev, device_id_type=MESH)

    def place(d):
        return z if d == 0 else nz - 1 - z

    def lower(d, s):
        return bits[s] == (0 if d == 0 else 1)

    def send_ctx(d, s, j):
        if s == nb - 1:
            @pl.when(lower(d, s))
            def _():
                state_copy(d, s, j).start()
        else:
            state_copy(d, s, j).start()

    def ctx_stage(d, s, j):
        state_copy(d, s - 1, j).wait_recv()
        snd[d, s, j] = (snd[d, s - 1, j].astype(F32) + rcv[d, s - 1, j].astype(F32)).astype(BF16)
        send_ctx(d, s, j)

    def ctx_last(d, j):
        total = jnp.zeros(u.shape[2:], F32)
        for s in range(nb - 1):
            total = total + jnp.where(lower(d, s), 0.0, rcv[d, s, j].astype(F32))
        u[d, j] = total

        @pl.when(jnp.logical_not(lower(d, nb - 1)))
        def _():
            state_copy(d, nb - 1, j).wait_recv()
            u[d, j] += rcv[d, nb - 1, j].astype(F32)

    def hop(d, i, j):
        p = place(d)

        @pl.when(p == i)
        def _():
            total = u[d, j] + snd[d, 0, j].astype(F32)
            if i > 0:
                state_copy(d, nb, j).wait_recv()
                total = total + rcv[d, nb, j].astype(F32)
            snd[d, nb, j] = total.astype(BF16)
            state_copy(d, nb, j).start()

        @pl.when(p == nz - 1 - i)
        def _():
            total = u[d, j]
            if i > 0:
                state_copy(d, nb + 1, j).wait_recv()
                total = total + rcv[d, nb + 1, j].astype(F32)
            snd[d, nb + 1, j] = total.astype(BF16)
            state_copy(d, nb + 1, j).start()

    def finish(d, j):
        p = place(d)

        @pl.when(p == nz - 1)
        def _():
            state_copy(d, nb, j).wait_recv()

        @pl.when(p == 0)
        def _():
            state_copy(d, nb + 1, j).wait_recv()

        @pl.when(p > 0)
        def _():
            u[d, j] += rcv[d, nb, j].astype(F32)

        @pl.when(p < nz - 1)
        def _():
            u[d, j] += rcv[d, nb + 1, j].astype(F32)

    lane = lax.broadcasted_iota(jnp.int32, (T, HD), 1)

    def causal():
        return lax.broadcasted_iota(jnp.int32, (T, T), 0) >= lax.broadcasted_iota(jnp.int32, (T, T), 1)

    def phi(x):
        return jnp.where(x > 0, x + 1.0, jnp.exp(jnp.minimum(x, 0.0)))

    def slope(x):
        return jnp.where(x > 0, 1.0, jnp.exp(jnp.minimum(x, 0.0)))

    def features(h, _):
        f = phi(k[:, cols(h)].astype(F32)).astype(BF16)
        fk[:, cols(h)] = f
        avec[pl.ds(h, 1), :] = jnp.sum(f.astype(F32), axis=0, keepdims=True)
        fq[:, cols(h)] = phi(q[:, cols(h)].astype(F32)).astype(BF16)
        return 0

    def first_s(j):
        for i in range(CH):
            h = j * CH + i
            snd[0, 0, j, i * HD:(i + 1) * HD, :] = dot(fk[:, cols(h)], v[:, cols(h)], 0, 0).astype(BF16)
        send_ctx(0, 0, j)

    def first_r(j):
        for i in range(CH):
            h = j * CH + i
            fqh = fq[:, cols(h)]
            scores = jnp.where(causal(), dot(fqh, fk[:, cols(h)], 1, 1), 0.0)
            w[h] = scores.astype(BF16)
            den = jnp.sum(scores, axis=1, keepdims=True) + jnp.sum(
                fqh.astype(F32) * zpre[pl.ds(h, 1), :], axis=1, keepdims=True)
            den_all[...] = jnp.where(lane == h, den, den_all[...])
            dnh = (g[:, cols(h)].astype(F32) / den).astype(BF16)
            dn[:, cols(h)] = dnh
            snd[1, 0, j, i * HD:(i + 1) * HD, :] = dot(fqh, dnh, 0, 0).astype(BF16)
        send_ctx(1, 0, j)

    def main_s(j):
        for i in range(CH):
            h = j * CH + i
            fqh = fq[:, cols(h)]
            fkh = fk[:, cols(h)]
            dnh = dn[:, cols(h)]
            state = u[0, j, i * HD:(i + 1) * HD, :].astype(BF16)
            den = jnp.sum(jnp.where(lane == h, den_all[...], 0.0), axis=1, keepdims=True)
            hh = dot(dnh, v[:, cols(h)], 1, 1)
            dd = dot(dnh, state, 1, 1)
            fqf = fqh.astype(F32)
            mass = jnp.sum(w[h].astype(F32) * hh, axis=1, keepdims=True) + jnp.sum(
                fqf * dd, axis=1, keepdims=True)
            dden = -mass / den
            gm = jnp.where(causal(), hh + dden, 0.0).astype(BF16)
            dfq = dot(gm, fkh, 1, 0) + dd + dden * zpre[pl.ds(h, 1), :]
            gq[:, cols(h)] = (dfq * slope(q[:, cols(h)].astype(F32))).astype(BF16)
            dfk[:, cols(h)] = dot(gm, fqh, 0, 0)
            cvec[pl.ds(h, 1), :] = jnp.sum(dden * fqf, axis=0, keepdims=True)

    def main_r(j):
        for i in range(CH):
            h = j * CH + i
            state = u[1, j, i * HD:(i + 1) * HD, :].astype(BF16)
            gv[:, cols(h)] = (dot(w[h], dn[:, cols(h)], 0, 0) + dot(fk[:, cols(h)], state, 1, 0)).astype(BF16)
            dfk[:, cols(h)] += dot(v[:, cols(h)], state, 1, 1)

    def last(h, _):
        total = dfk[:, cols(h)] + rpre[pl.ds(h, 1), :]
        gk[:, cols(h)] = (total * slope(k[:, cols(h)].astype(F32))).astype(BF16)
        return 0

    den_all[...] = jnp.ones((T, HD), F32)
    lax.fori_loop(0, H, features, 0)
    vec_start(0, avec)

    def step(t, _):
        def at(off, fn):
            j = t - off

            @pl.when((j >= 0) & (j < NC))
            def _():
                fn(j)

        at(0, first_s)

        @pl.when(t == VB)
        def _():
            vec_middle(0, avec, zpre)

        @pl.when(t == VC)
        def _():
            vec_end(0, avec, zpre)

        at(D1, first_r)

        @pl.when(t == NS + NC)
        def _():
            vec_start(1, cvec)

        @pl.when(t == NS + NC + 1)
        def _():
            vec_middle(1, cvec, rpre)

        for d, base in ((0, 0), (1, D1)):
            for s in range(1, nb):
                at(base + s, functools.partial(ctx_stage, d, s))
            at(base + nb, functools.partial(ctx_last, d))
            for i in range(nz - 1):
                at(base + nb + i, functools.partial(hop, d, i))
            at(base + NS, functools.partial(finish, d))
        at(NS, main_s)
        at(D1 + NS, main_r)
        return 0

    lax.fori_loop(0, D1 + NS + NC, step, 0)
    vec_end(1, cvec, rpre)
    lax.fori_loop(0, H, last, 0)

    for d, src in ((0, avec), (1, cvec)):
        for o in range(1, nctx):
            vec_ctx(d, o, src).wait_send()
        for o in range(1, nz):
            vec_z(d, o, 0).wait_send()

    def drain(j, _):
        for d in range(2):
            for s in range(nb - 1):
                state_copy(d, s, j).wait_send()

            @pl.when(lower(d, nb - 1))
            def _():
                state_copy(d, nb - 1, j).wait_send()

            @pl.when(place(d) < nz - 1)
            def _():
                state_copy(d, nb, j).wait_send()

            @pl.when(place(d) > 0)
            def _():
                state_copy(d, nb + 1, j).wait_send()
        return 0

    lax.fori_loop(0, NC, drain, 0)


def solution(mesh):
    nctx, nz = mesh.shape["ctx"], mesh.shape["head"]

    def shards(queries, keys, values, out_grad):
        T, width = queries.shape
        H = width // HD
        NC = H // CH
        nb = nctx.bit_length() - 1
        rows = CH * HD
        whole = jax.ShapeDtypeStruct((T, width), BF16)
        dma = pltpu.SemaphoreType.DMA
        return pl.pallas_call(
            functools.partial(kernel, nctx, nz),
            out_shape=(whole, whole, whole),
            in_specs=[pl.BlockSpec(memory_space=pltpu.VMEM)] * 4,
            out_specs=[pl.BlockSpec(memory_space=pltpu.VMEM)] * 3,
            scratch_shapes=[
                pltpu.VMEM((T, width), BF16),
                pltpu.VMEM((T, width), BF16),
                pltpu.VMEM((T, width), BF16),
                pltpu.VMEM((H, T, T), BF16),
                pltpu.VMEM((T, width), F32),
                pltpu.VMEM((T, HD), F32),
                pltpu.VMEM((2, NC, rows, HD), F32),
                pltpu.VMEM((2, nb + 2, NC, rows, HD), BF16),
                pltpu.VMEM((2, nb + 2, NC, rows, HD), BF16),
                pltpu.VMEM((H, HD), F32),
                pltpu.VMEM((H, HD), F32),
                pltpu.VMEM((H, HD), F32),
                pltpu.VMEM((H, HD), F32),
                pltpu.VMEM((2, nctx, H, HD), F32),
                pltpu.VMEM((2, 2, H, HD), F32),
                pltpu.VMEM((2, nz, H, HD), F32),
                dma((2, nb + 2, NC)),
                dma((2, nb + 2, NC)),
                dma((2, nctx)),
                dma((2, nctx)),
                dma((2, nz)),
                dma((2, nz)),
            ],
            compiler_params=pltpu.CompilerParams(
                collective_id=0, has_side_effects=True, vmem_limit_bytes=62 * 1024 * 1024
            ),
        )(queries, keys, values, out_grad)

    spec = P(("ctx", "head"), None)
    return jax.shard_map(
        shards, mesh=mesh, in_specs=(spec,) * 4, out_specs=(spec,) * 3, check_vma=False
    )
```

```python
import functools

import jax
import jax.numpy as jnp
from jax import lax
from jax.experimental import pallas as pl
from jax.experimental.pallas import tpu as pltpu
from jax.sharding import PartitionSpec as P

HD = 128
CH = 2
F32 = jnp.float32
BF16 = jnp.bfloat16
MESH = pl.DeviceIdType.MESH


def dot(a, b, ca, cb):
    return lax.dot_general(a, b, (((ca,), (cb,)), ((), ())), preferred_element_type=F32)


def kernel(nctx, nz, q, k, v, g, gq, gk, gv, fq, fk, dn, w, dfk, u, snd, rcv,
           avec, zpre, cvec, rpre, vrcv, zsnd, zrcv, ss, rs, vss, vrs, zss, zrs):
    T = q.shape[0]
    H = q.shape[1] // HD
    NC = H // CH
    nb = nctx.bit_length() - 1
    NS = nb + nz - 1
    VB, VC, D1 = 2, 4, 6
    LAG = 2
    OFF = [0] + [1 + LAG * i for i in range(NS)]
    END = OFF[NS]
    c = lax.axis_index("ctx")
    z = lax.axis_index("head")

    barrier = pltpu.get_barrier_semaphore()
    for o in range(1, nctx):
        pl.semaphore_signal(barrier, inc=1, device_id=(lax.rem(c + o, nctx), z), device_id_type=MESH)
    for o in range(1, nz):
        pl.semaphore_signal(barrier, inc=1, device_id=(c, lax.rem(z + o, nz)), device_id_type=MESH)
    pl.semaphore_wait(barrier, nctx + nz - 2)

    bits = [lax.rem(c // (1 << s), 2) for s in range(nb)]

    def cols(h):
        return pl.ds(pl.multiple_of(h * HD, HD), HD)

    def vec_ctx(d, o, src):
        return pltpu.make_async_remote_copy(
            src_ref=src, dst_ref=vrcv.at[d, c], send_sem=vss.at[d, o], recv_sem=vrs.at[d, c],
            device_id=(lax.rem(c + o, nctx), z), device_id_type=MESH)

    def vec_ctx_from(d, o, src):
        p = lax.rem(c + o, nctx)
        return p, pltpu.make_async_remote_copy(
            src_ref=src, dst_ref=vrcv.at[d, p], send_sem=vss.at[d, o], recv_sem=vrs.at[d, p],
            device_id=(p, z), device_id_type=MESH)

    def vec_z(d, o, which):
        return pltpu.make_async_remote_copy(
            src_ref=zsnd.at[d, which], dst_ref=zrcv.at[d, z], send_sem=zss.at[d, o], recv_sem=zrs.at[d, z],
            device_id=(c, lax.rem(z + o, nz)), device_id_type=MESH)

    def vec_z_from(d, o):
        p = lax.rem(z + o, nz)
        return p, pltpu.make_async_remote_copy(
            src_ref=zsnd.at[d, 0], dst_ref=zrcv.at[d, p], send_sem=zss.at[d, o], recv_sem=zrs.at[d, p],
            device_id=(c, p), device_id_type=MESH)

    def vec_start(d, src):
        for o in range(1, nctx):
            vec_ctx(d, o, src).start()

    def vec_middle(d, src, out):
        total = jnp.zeros((H, HD), F32)
        for o in range(1, nctx):
            p, copy = vec_ctx_from(d, o, src)
            copy.wait_recv()
            take = (p < c) if d == 0 else (p > c)
            total = total + jnp.where(take, vrcv[d, p], 0.0)
        out[...] = total
        zsnd[d, 0] = total + src[...]
        zsnd[d, 1] = total
        for o in range(1, nz):
            ahead = lax.rem(z + o, nz) > z
            which = jnp.where(ahead, 0, 1) if d == 0 else jnp.where(ahead, 1, 0)
            vec_z(d, o, which).start()

    def vec_end(d, src, out):
        total = out[...]
        for o in range(1, nz):
            p, copy = vec_z_from(d, o)
            copy.wait_recv()
            total = total + zrcv[d, p]
        out[...] = total

    def state_copy(d, s, j):
        if s < nb:
            dev = (c + (1 - 2 * bits[s]) * (1 << s), z)
        else:
            up = (s == nb) == (d == 0)
            dev = (c, jnp.clip(z + 1, 0, nz - 1) if up else jnp.clip(z - 1, 0, nz - 1))
        return pltpu.make_async_remote_copy(
            src_ref=snd.at[d, s, j], dst_ref=rcv.at[d, s, j], send_sem=ss.at[d, s, j],
            recv_sem=rs.at[d, s, j], device_id=dev, device_id_type=MESH)

    def place(d):
        return z if d == 0 else nz - 1 - z

    def lower(d, s):
        return bits[s] == (0 if d == 0 else 1)

    def send_ctx(d, s, j):
        if s == nb - 1:
            @pl.when(lower(d, s))
            def _():
                state_copy(d, s, j).start()
        else:
            state_copy(d, s, j).start()

    def ctx_stage(d, s, j):
        state_copy(d, s - 1, j).wait_recv()
        snd[d, s, j] = (snd[d, s - 1, j].astype(F32) + rcv[d, s - 1, j].astype(F32)).astype(BF16)
        send_ctx(d, s, j)

    def ctx_last(d, j):
        total = jnp.zeros(u.shape[2:], F32)
        for s in range(nb - 1):
            total = total + jnp.where(lower(d, s), 0.0, rcv[d, s, j].astype(F32))
        u[d, j] = total

        @pl.when(jnp.logical_not(lower(d, nb - 1)))
        def _():
            state_copy(d, nb - 1, j).wait_recv()
            u[d, j] += rcv[d, nb - 1, j].astype(F32)

    def hop(d, i, j):
        p = place(d)

        @pl.when(p == i)
        def _():
            total = u[d, j] + snd[d, 0, j].astype(F32)
            if i > 0:
                state_copy(d, nb, j).wait_recv()
                total = total + rcv[d, nb, j].astype(F32)
            snd[d, nb, j] = total.astype(BF16)
            state_copy(d, nb, j).start()

        @pl.when(p == nz - 1 - i)
        def _():
            total = u[d, j]
            if i > 0:
                state_copy(d, nb + 1, j).wait_recv()
                total = total + rcv[d, nb + 1, j].astype(F32)
            snd[d, nb + 1, j] = total.astype(BF16)
            state_copy(d, nb + 1, j).start()

    def finish(d, j):
        p = place(d)

        @pl.when(p == nz - 1)
        def _():
            state_copy(d, nb, j).wait_recv()

        @pl.when(p == 0)
        def _():
            state_copy(d, nb + 1, j).wait_recv()

        @pl.when(p > 0)
        def _():
            u[d, j] += rcv[d, nb, j].astype(F32)

        @pl.when(p < nz - 1)
        def _():
            u[d, j] += rcv[d, nb + 1, j].astype(F32)

    def causal():
        return lax.broadcasted_iota(jnp.int32, (T, T), 0) >= lax.broadcasted_iota(jnp.int32, (T, T), 1)

    def phi(x):
        return jnp.where(x > 0, x + 1.0, jnp.exp(jnp.minimum(x, 0.0)))

    def slope(x):
        return jnp.where(x > 0, 1.0, jnp.exp(jnp.minimum(x, 0.0)))

    def features(h, _):
        f = phi(k[:, cols(h)].astype(F32)).astype(BF16)
        fk[:, cols(h)] = f
        avec[pl.ds(h, 1), :] = jnp.sum(f.astype(F32), axis=0, keepdims=True)
        fq[:, cols(h)] = phi(q[:, cols(h)].astype(F32)).astype(BF16)
        return 0

    def first_s(j):
        for i in range(CH):
            h = j * CH + i
            snd[0, 0, j, i * HD:(i + 1) * HD, :] = dot(fk[:, cols(h)], v[:, cols(h)], 0, 0).astype(BF16)
        send_ctx(0, 0, j)

    def first_r(j):
        for i in range(CH):
            h = j * CH + i
            fqh = fq[:, cols(h)]
            scores = jnp.where(causal(), dot(fqh, fk[:, cols(h)], 1, 1), 0.0)
            w[h] = scores.astype(BF16)
            den = jnp.sum(fold(scores) + fqh.astype(F32) * zpre[pl.ds(h, 1), :], axis=1, keepdims=True)
            inv = jnp.broadcast_to(1.0 / den, (T, HD))
            dfk[:, cols(h)] = inv
            dnh = (g[:, cols(h)].astype(F32) * inv).astype(BF16)
            dn[:, cols(h)] = dnh
            snd[1, 0, j, i * HD:(i + 1) * HD, :] = dot(fqh, dnh, 0, 0).astype(BF16)
        send_ctx(1, 0, j)

    def fold(x):
        total = x[:, :HD]
        for o in range(HD, T, HD):
            total = total + x[:, o:o + HD]
        return total

    def main_s(j):
        for i in range(CH):
            h = j * CH + i
            fqh = fq[:, cols(h)]
            fkh = fk[:, cols(h)]
            dnh = dn[:, cols(h)]
            state = u[0, j, i * HD:(i + 1) * HD, :].astype(BF16)
            hh = dot(dnh, v[:, cols(h)], 1, 1)
            dd = dot(dnh, state, 1, 1)
            fqf = fqh.astype(F32)
            mass = jnp.sum(fold(w[h].astype(F32) * hh) + fqf * dd, axis=1, keepdims=True)
            dden = -mass * dfk[:, cols(h)][:, :1]
            gm = jnp.where(causal(), hh + dden, 0.0).astype(BF16)
            dfq = dot(gm, fkh, 1, 0) + dd + dden * zpre[pl.ds(h, 1), :]
            gq[:, cols(h)] = (dfq * slope(q[:, cols(h)].astype(F32))).astype(BF16)
            dfk[:, cols(h)] = dot(gm, fqh, 0, 0)
            cvec[pl.ds(h, 1), :] = jnp.sum(dden * fqf, axis=0, keepdims=True)

    def main_r(j):
        for i in range(CH):
            h = j * CH + i
            state = u[1, j, i * HD:(i + 1) * HD, :].astype(BF16)
            gv[:, cols(h)] = (dot(w[h], dn[:, cols(h)], 0, 0) + dot(fk[:, cols(h)], state, 1, 0)).astype(BF16)
            dfk[:, cols(h)] += dot(v[:, cols(h)], state, 1, 1)

    def last(h, _):
        total = dfk[:, cols(h)] + rpre[pl.ds(h, 1), :]
        gk[:, cols(h)] = (total * slope(k[:, cols(h)].astype(F32))).astype(BF16)
        return 0

    lax.fori_loop(0, H, features, 0)
    vec_start(0, avec)

    def step(t, _):
        def at(off, fn):
            j = t - off

            @pl.when((j >= 0) & (j < NC))
            def _():
                fn(j)

        at(0, first_s)

        @pl.when(t == VB)
        def _():
            vec_middle(0, avec, zpre)

        @pl.when(t == VC)
        def _():
            vec_end(0, avec, zpre)

        at(D1, first_r)

        @pl.when(t == END + NC)
        def _():
            vec_start(1, cvec)

        @pl.when(t == END + NC + 1)
        def _():
            vec_middle(1, cvec, rpre)

        for d, base in ((0, 0), (1, D1)):
            for s in range(1, nb):
                at(base + OFF[s], functools.partial(ctx_stage, d, s))
            at(base + OFF[nb], functools.partial(ctx_last, d))
            for i in range(nz - 1):
                at(base + OFF[nb + i], functools.partial(hop, d, i))
            at(base + END, functools.partial(finish, d))
        at(END, main_s)
        at(D1 + END, main_r)
        return 0

    lax.fori_loop(0, D1 + END + NC, step, 0)
    vec_end(1, cvec, rpre)
    lax.fori_loop(0, H, last, 0)

    for d, src in ((0, avec), (1, cvec)):
        for o in range(1, nctx):
            vec_ctx(d, o, src).wait_send()
        for o in range(1, nz):
            vec_z(d, o, 0).wait_send()

    def drain(j, _):
        for d in range(2):
            for s in range(nb - 1):
                state_copy(d, s, j).wait_send()

            @pl.when(lower(d, nb - 1))
            def _():
                state_copy(d, nb - 1, j).wait_send()

            @pl.when(place(d) < nz - 1)
            def _():
                state_copy(d, nb, j).wait_send()

            @pl.when(place(d) > 0)
            def _():
                state_copy(d, nb + 1, j).wait_send()
        return 0

    lax.fori_loop(0, NC, drain, 0)


def solution(mesh):
    nctx, nz = mesh.shape["ctx"], mesh.shape["head"]

    def shards(queries, keys, values, out_grad):
        T, width = queries.shape
        H = width // HD
        NC = H // CH
        nb = nctx.bit_length() - 1
        rows = CH * HD
        whole = jax.ShapeDtypeStruct((T, width), BF16)
        dma = pltpu.SemaphoreType.DMA
        return pl.pallas_call(
            functools.partial(kernel, nctx, nz),
            out_shape=(whole, whole, whole),
            in_specs=[pl.BlockSpec(memory_space=pltpu.VMEM)] * 4,
            out_specs=[pl.BlockSpec(memory_space=pltpu.VMEM)] * 3,
            scratch_shapes=[
                pltpu.VMEM((T, width), BF16),
                pltpu.VMEM((T, width), BF16),
                pltpu.VMEM((T, width), BF16),
                pltpu.VMEM((H, T, T), BF16),
                pltpu.VMEM((T, width), F32),
                pltpu.VMEM((2, NC, rows, HD), F32),
                pltpu.VMEM((2, nb + 2, NC, rows, HD), BF16),
                pltpu.VMEM((2, nb + 2, NC, rows, HD), BF16),
                pltpu.VMEM((H, HD), F32),
                pltpu.VMEM((H, HD), F32),
                pltpu.VMEM((H, HD), F32),
                pltpu.VMEM((H, HD), F32),
                pltpu.VMEM((2, nctx, H, HD), F32),
                pltpu.VMEM((2, 2, H, HD), F32),
                pltpu.VMEM((2, nz, H, HD), F32),
                dma((2, nb + 2, NC)),
                dma((2, nb + 2, NC)),
                dma((2, nctx)),
                dma((2, nctx)),
                dma((2, nz)),
                dma((2, nz)),
            ],
            compiler_params=pltpu.CompilerParams(
                collective_id=0, has_side_effects=True, vmem_limit_bytes=62 * 1024 * 1024
            ),
        )(queries, keys, values, out_grad)

    spec = P(("ctx", "head"), None)
    return jax.shard_map(
        shards, mesh=mesh, in_specs=(spec,) * 4, out_specs=(spec,) * 3, check_vma=False
    )
```
